32 devices in a mesh: blk: 16 (over z, y, x), grp: 2 (over core).
Axes of the slice: x: 2, y: 2, z: 4, core: 2. Of those that a mesh axis runs over, the one named last changes fastest.
Arguments:
- rhs: float32 [4, 16, 128, 128], P(None, 'blk', 'grp'), may hold values from -6 to 6
- diag_inv: bfloat16 [4, 16, 128, 128], P(None, 'blk'), as said below
- off_blocks: bfloat16 [3, 16, 4, 128, 128], P(None, 'blk'), may hold values from -0.25 to 0.25
- columns: int32 [3, 16, 4], P(None, 'blk'), may hold values from 0 to 47, as said below
- owner: int32 [4, 16], replicated, may hold values from 0 to 15, each once within a row
- train_desc: bfloat16 [4, 16, 128, 1024], P(None, 'blk'), may hold values from -6 to 6
- pred_desc: bfloat16 [2, 512, 1024], P('grp'), may hold values from -6 to 6
Outputs:
- solved: bfloat16 [4, 16, 128, 128], P(None, 'blk', 'grp')
- predicted: float32 [2, 512, 128], P('grp', 'blk')
The draws below stay inside these ranges and needn't reach their ends.
Inputs may be any that keep to these rules, and one draw needn't show every extreme that they name: `columns`: the 4 numbers of a block row of level l (array index l - 1) are distinct block-row numbers of levels below l, that is below l * 16. Each row of owner is a permutation of the device indices along blk. `diag_inv`: each block is zero below its diagonal.
All inputs are finite; a program needn't handle non-finite values.
Results may differ from the reference program's by a relative error of at most 0.007.
Values may be sent and summed in bfloat16 or wider, within the bound.
A program may use at most 128 MiB of HBM per device.

```python
import math
import jax
import jax.numpy as jnp
from jax import lax

BS = 128
LEVELS = 4
KB = 4
RHS = 128
F = 1024
LVL = 16
HALVES = 2
PRED_G = 512


def draw_diag_inv(key, part):
    key_diag, key_off = jax.random.split(jax.random.fold_in(key, 11))
    shape = (LEVELS, LVL, BS, BS)
    diag_vals = jax.random.uniform(key_diag, (LEVELS, LVL, BS), jnp.float32, 0.6, 1.2)
    off_vals = jax.random.normal(key_off, shape, jnp.float32) * (0.5 / math.sqrt(BS))
    row_index = jnp.arange(BS)[:, None]
    col_index = jnp.arange(BS)[None, :]
    upper_mask = (row_index < col_index).astype(jnp.float32)
    identity = jnp.eye(BS, dtype=jnp.float32)
    return (off_vals * upper_mask + identity * diag_vals[..., None]).astype(jnp.bfloat16)


def draw_columns(key, part):
    rows_list = []
    for level in range(1, LEVELS):
        keys = jax.random.split(jax.random.fold_in(key, 100 + level), LVL)
        picks = jax.vmap(lambda one_key: jax.random.permutation(one_key, level * LVL)[:KB])(keys)
        picks = picks.astype(jnp.int32)
        if level == 1:
            picks = picks.at[0].set(jnp.arange(KB, dtype=jnp.int32))
        if level == LEVELS - 1:
            picks = picks.at[LVL - 1].set((level * LVL - 1 - jnp.arange(KB)).astype(jnp.int32))
        rows_list.append(picks)
    return jnp.stack(rows_list)


def shard_levels(stream_key, extent, cuts, least, top_value):
    gain, own = 1.0, jax.random.fold_in(stream_key, 6)
    for dim, shards_of in cuts:
        steps = jnp.exp(jax.random.uniform(jax.random.fold_in(own, dim), (shards_of,), jnp.float32, least / len(cuts), top_value / len(cuts)))
        gain = gain * jnp.repeat(steps, extent[dim] // shards_of).reshape([-1 if axis == dim else 1 for axis in range(len(extent))])
    return gain


def gaussian(rng, shape, width, reach, cuts=(), kind=jnp.bfloat16):
    array = width * jax.random.normal(rng, shape, jnp.float32)
    if cuts:
        array = array * shard_levels(rng, shape, cuts, -0.22, 0.18)
    return jnp.clip(array, -reach, reach).astype(kind)


def setup_inputs(seed: int = 0) -> dict:
    splits = jax.random.split(jax.random.key(seed), 8)
    return {
        "rhs": gaussian(splits[0], (LEVELS, LVL, RHS, BS), 1.0, 6.0, ((1, 16), (2, 2)), jnp.float32),
        "diag_inv": draw_diag_inv(jax.random.fold_in(splits[7], 71), 0),
        "off_blocks": gaussian(splits[2], (LEVELS - 1, LVL, KB, BS, BS), (KB * BS) ** -0.5, 0.25, ((1, 16),)),
        "columns": draw_columns(jax.random.fold_in(splits[7], 71), 0),
        "owner": jax.vmap(lambda own: jax.random.permutation(own, LVL))(jax.random.split(splits[4], LEVELS)).reshape((LEVELS, LVL)).astype(jnp.int32),
        "train_desc": gaussian(splits[5], (LEVELS, LVL, BS, F), 1.0, 6.0, ((1, 16),)),
        "pred_desc": gaussian(splits[6], (HALVES, PRED_G, F), 1.0, 6.0, ((0, 2),)),
    }


def reference(rhs, diag_inv, off_blocks, columns, owner, train_desc, pred_desc):
    panels = []
    for level in range(LEVELS):
        partial_rhs = rhs[level]
        if level > 0:
            flat = jnp.concatenate(panels, axis=0)
            wanted = columns[level - 1]
            which_level = wanted // LVL
            position = (which_level * LVL + owner[which_level, wanted % LVL]).astype(jnp.int32)
            picked = flat[position].astype(jnp.float32)
            partial_rhs = partial_rhs - jnp.einsum("mkrs,mkst->mrt", picked, off_blocks[level - 1].astype(jnp.float32))
        rounded = lax.optimization_barrier(partial_rhs.astype(jnp.bfloat16)).astype(jnp.float32)
        solved_level = jnp.einsum("mrs,mst->mrt", rounded, diag_inv[level].astype(jnp.float32)).astype(jnp.bfloat16)
        panels.append(solved_level)
    solved = jnp.stack(panels)
    train_flat = train_desc.astype(jnp.float32).reshape(LEVELS * LVL * BS, F)
    values = jnp.transpose(solved.astype(jnp.float32), (0, 1, 3, 2)).reshape(LEVELS * LVL * BS, RHS)
    rows_total = HALVES * PRED_G
    step_rows = math.gcd(rows_total, 512)
    queries = pred_desc.astype(jnp.float32).reshape(rows_total // step_rows, step_rows, F)

    def one_block(block_queries):
        inner = jnp.dot(block_queries, train_flat.T)
        scaled = inner / F
        table = lax.optimization_barrier((scaled * scaled).astype(jnp.bfloat16)).astype(jnp.float32)
        return jnp.dot(table, values)

    predicted = lax.map(one_block, queries).reshape(HALVES, PRED_G, RHS)
    return solved, predicted
```

```python
import functools

import jax
import jax.numpy as jnp
from jax import lax
from jax.experimental import pallas as pl
from jax.experimental.pallas import tpu as pltpu
from jax.sharding import PartitionSpec as P

F32 = jnp.float32
BF16 = jnp.bfloat16
CONTRACT_LAST = (((1,), (1,)), ((), ()))


def kernel(n, levels, columns_ref, owner_ref, rhs_ref, diag_ref, off_ref, train_hbm, pred_hbm,
           solved_ref, predicted_ref, *scratch):
    stores = scratch[: levels - 1]
    (full, train, pred, table, acc, outbox, inbox, pick_rows,
     local_sem, send_sem, recv_sem, pair_send, pair_recv, sum_send, sum_recv) = scratch[levels - 1:]
    me = lax.axis_index("blk")
    half = lax.axis_index("grp")
    rows, bs = rhs_ref.shape[1], rhs_ref.shape[2]
    width = train.shape[1]
    block_rows = outbox.shape[1]
    own_rows = predicted_ref.shape[0]

    load_train = pltpu.make_async_copy(train_hbm, train, local_sem.at[0])
    load_pred = pltpu.make_async_copy(pred_hbm, pred, local_sem.at[1])
    load_train.start()
    load_pred.start()

    barrier = pltpu.get_barrier_semaphore()

    def greet(step, carry):
        pl.semaphore_signal(barrier, inc=1, device_id={"blk": lax.rem(me + step, n)},
                            device_id_type=pl.DeviceIdType.MESH)
        return carry

    lax.fori_loop(1, n, greet, 0)
    pl.semaphore_signal(barrier, inc=1, device_id={"grp": 1 - half}, device_id_type=pl.DeviceIdType.MESH)

    def panel_copy(level, peer):
        return pltpu.make_async_remote_copy(
            src_ref=stores[level].at[me], dst_ref=stores[level].at[me],
            send_sem=send_sem.at[level], recv_sem=recv_sem.at[level],
            device_id={"blk": peer}, device_id_type=pl.DeviceIdType.MESH)

    def all_panels(level):
        every = stores[level].at[pl.ds(0, n - 1)]
        return pltpu.make_async_remote_copy(
            src_ref=every, dst_ref=every,
            send_sem=send_sem.at[level], recv_sem=recv_sem.at[level],
            device_id={"blk": lax.rem(me + 1, n)}, device_id_type=pl.DeviceIdType.MESH)

    def pair_copy(level):
        return pltpu.make_async_remote_copy(
            src_ref=full.at[level, half], dst_ref=full.at[level, half],
            send_sem=pair_send.at[level], recv_sem=pair_recv.at[level],
            device_id={"grp": 1 - half}, device_id_type=pl.DeviceIdType.MESH)

    def add_level(level):
        pair_copy(level).wait_recv()
        panel = full[level].reshape(2 * rows, bs)
        part = lax.dot_general(table[:, level * bs:(level + 1) * bs], panel, CONTRACT_LAST,
                               preferred_element_type=F32)
        part = part.reshape(acc.shape)
        acc[...] = part if level == 0 else acc[...] + part

    for level in range(levels):
        partial_rhs = rhs_ref[level]
        if level > 0:
            all_panels(level - 1).wait_recv()
            picks = []
            for k in range(columns_ref.shape[1]):
                wanted = columns_ref[level - 1, k]
                from_level = wanted // n
                place = owner_ref[from_level, lax.rem(wanted, n)]
                panel = stores[0][place]
                for other in range(1, level):
                    panel = jnp.where(from_level == other, stores[other][place], panel)
                picks.append(panel)
            partial_rhs = partial_rhs - jnp.dot(
                jnp.concatenate(picks, axis=1), off_ref[level - 1], preferred_element_type=F32)
        panel = jnp.dot(partial_rhs.astype(BF16), diag_ref[level], preferred_element_type=F32).astype(BF16)
        solved_ref[level] = panel
        full[level, half] = panel
        if level + 1 < levels:
            stores[level][me] = panel
        if level == 0:
            pl.semaphore_wait(barrier, n)
        if level + 1 < levels:

            def send_panel(step, carry):
                panel_copy(level, lax.rem(me + step, n)).start()
                return carry

            lax.fori_loop(1, n, send_panel, 0)
        pair_copy(level).start()
        if level == 0:
            load_train.wait()
            load_pred.wait()
            inner = lax.dot_general(pred[...], train[...], CONTRACT_LAST, preferred_element_type=F32)
            inner = inner / width
            table[...] = (inner * inner).astype(BF16)
        add_level(level)

    outbox[...] = acc[...].astype(BF16)

    def sum_copy(peer):
        return pltpu.make_async_remote_copy(
            src_ref=outbox.at[peer * own_rows // block_rows], dst_ref=inbox.at[me],
            send_sem=sum_send, recv_sem=sum_recv,
            device_id={"blk": peer}, device_id_type=pl.DeviceIdType.MESH)

    inbox[me] = jnp.zeros(inbox.shape[1:], BF16)

    def send_sum(step, carry):
        sum_copy(lax.rem(me + step, n)).start()
        return carry

    lax.fori_loop(1, n, send_sum, 0)
    every = inbox.at[pl.ds(0, n - 1)]
    sums = pltpu.make_async_remote_copy(
        src_ref=every, dst_ref=every, send_sem=sum_send, recv_sem=sum_recv,
        device_id={"blk": lax.rem(me + 1, n)}, device_id_type=pl.DeviceIdType.MESH)
    for level in range(levels):
        pair_copy(level).wait_send()
        if level + 1 < levels:
            all_panels(level).wait_send()
    sums.wait_recv()
    total = acc[me * own_rows // block_rows] + jnp.sum(inbox[...].astype(F32), axis=0)
    if own_rows == block_rows:
        predicted_ref[...] = total
    else:
        pick_rows[...] = total
        predicted_ref[...] = pick_rows[pl.ds(lax.rem(me * own_rows, block_rows), own_rows)]
    sums.wait_send()


def body(rhs, diag_inv, off_blocks, columns, owner, train_desc, pred_desc):
    levels, _, rows, bs = rhs.shape
    n = lax.axis_size("blk")
    kb = columns.shape[2]
    features = train_desc.shape[3]
    queries = pred_desc.shape[1]
    own_rows = queries // n
    block_rows = max(own_rows, 16)
    vmem = pl.BlockSpec(memory_space=pltpu.VMEM)
    smem = pl.BlockSpec(memory_space=pltpu.SMEM)
    hbm = pl.BlockSpec(memory_space=pl.ANY)
    solved, predicted = pl.pallas_call(
        functools.partial(kernel, n, levels),
        out_shape=(
            jax.ShapeDtypeStruct((levels, rows, bs), BF16),
            jax.ShapeDtypeStruct((own_rows, 2 * rows), F32),
        ),
        in_specs=[smem, smem, vmem, vmem, vmem, hbm, hbm],
        out_specs=(vmem, vmem),
        scratch_shapes=[pltpu.VMEM((n, rows, bs), BF16) for _ in range(levels - 1)] + [
            pltpu.VMEM((levels, 2, rows, bs), BF16),
            pltpu.VMEM((levels * bs, features), BF16),
            pltpu.VMEM((queries, features), BF16),
            pltpu.VMEM((queries, levels * bs), BF16),
            pltpu.VMEM((queries // block_rows, block_rows, 2 * rows), F32),
            pltpu.VMEM((queries // block_rows, block_rows, 2 * rows), BF16),
            pltpu.VMEM((n, block_rows, 2 * rows), BF16),
            pltpu.VMEM((block_rows, 2 * rows), F32),
            pltpu.SemaphoreType.DMA((2,)),
            pltpu.SemaphoreType.DMA((levels,)),
            pltpu.SemaphoreType.DMA((levels,)),
            pltpu.SemaphoreType.DMA((levels,)),
            pltpu.SemaphoreType.DMA((levels,)),
            pltpu.SemaphoreType.DMA,
            pltpu.SemaphoreType.DMA,
        ],
        compiler_params=pltpu.CompilerParams(
            collective_id=0, has_side_effects=True, vmem_limit_bytes=50 * 1024 * 1024),
    )(
        columns[:, 0], owner, rhs[:, 0], diag_inv[:, 0],
        off_blocks.reshape(levels - 1, kb * bs, bs),
        train_desc.reshape(levels * bs, features), pred_desc[0],
    )
    return solved[:, None], predicted[None]


def solution(mesh):
    placed = (
        P(None, "blk", "grp", None),
        P(None, "blk", None, None),
        P(None, "blk", None, None, None),
        P(None, "blk", None),
        P(),
        P(None, "blk", None, None),
        P("grp", None, None),
    )
    return jax.shard_map(
        body,
        mesh=mesh,
        in_specs=placed,
        out_specs=(P(None, "blk", "grp", None), P("grp", "blk", None)),
        check_vma=False,
    )
```

```python
import functools

import jax
import jax.numpy as jnp
from jax import lax
from jax.experimental import pallas as pl
from jax.experimental.pallas import tpu as pltpu
from jax.sharding import PartitionSpec as P

F32 = jnp.float32
BF16 = jnp.bfloat16
CONTRACT_LAST = (((1,), (1,)), ((), ()))


def kernel(n, levels, *refs):
    operands, (solved_ref, predicted_ref), scratch = refs[:7], refs[7:9], refs[9:]
    stores = scratch[: levels - 1]
    (rhs_ref, diag_ref, columns_ref, owner_ref, off_ref, pred, train,
     full, table, acc, outbox, inbox, pick_rows,
     local_sem, send_sem, recv_sem, pair_send, pair_recv, sum_send, sum_recv) = scratch[levels - 1:]
    me = lax.axis_index("blk")
    half = lax.axis_index("grp")
    rows, bs = rhs_ref.shape[2], rhs_ref.shape[3]
    width = train.shape[1]
    kb = columns_ref.shape[2]
    block_rows = outbox.shape[1]
    own_rows = predicted_ref.shape[1]

    here = (rhs_ref, diag_ref, columns_ref, owner_ref, off_ref, pred, train)
    loads = [pltpu.make_async_copy(operand, local, local_sem.at[i])
             for i, (operand, local) in enumerate(zip(operands, here))]
    for load in loads:
        load.start()

    barrier = pltpu.get_barrier_semaphore()

    def greet(step, carry):
        pl.semaphore_signal(barrier, inc=1, device_id={"blk": lax.rem(me + step, n)},
                            device_id_type=pl.DeviceIdType.MESH)
        return carry

    lax.fori_loop(1, n, greet, 0)
    pl.semaphore_signal(barrier, inc=1, device_id={"grp": 1 - half}, device_id_type=pl.DeviceIdType.MESH)

    def panel_copy(level, peer):
        return pltpu.make_async_remote_copy(
            src_ref=stores[level].at[me], dst_ref=stores[level].at[me],
            send_sem=send_sem.at[level], recv_sem=recv_sem.at[level],
            device_id={"blk": peer}, device_id_type=pl.DeviceIdType.MESH)

    def all_panels(level):
        every = stores[level].at[pl.ds(0, n - 1)]
        return pltpu.make_async_remote_copy(
            src_ref=every, dst_ref=every,
            send_sem=send_sem.at[level], recv_sem=recv_sem.at[level],
            device_id={"blk": lax.rem(me + 1, n)}, device_id_type=pl.DeviceIdType.MESH)

    def pair_copy(level):
        return pltpu.make_async_remote_copy(
            src_ref=full.at[level, half], dst_ref=full.at[level, half],
            send_sem=pair_send.at[level], recv_sem=pair_recv.at[level],
            device_id={"grp": 1 - half}, device_id_type=pl.DeviceIdType.MESH)

    def add_level(level):
        pair_copy(level).wait_recv()
        panel = full[level].reshape(2 * rows, bs)
        part = lax.dot_general(table[:, level * bs:(level + 1) * bs], panel, CONTRACT_LAST,
                               preferred_element_type=F32)
        part = part.reshape(acc.shape)
        acc[...] = part if level == 0 else acc[...] + part

    for level in range(levels):
        if level == 0:
            loads[0].wait()
            loads[1].wait()
        partial_rhs = rhs_ref[level, 0]
        if level > 0:
            all_panels(level - 1).wait_recv()
            picks = []
            for k in range(kb):
                wanted = columns_ref[level - 1, 0, k]
                from_level = wanted // n
                place = owner_ref[from_level, lax.rem(wanted, n)]
                panel = stores[0][place]
                for other in range(1, level):
                    panel = jnp.where(from_level == other, stores[other][place], panel)
                picks.append(panel)
            partial_rhs = partial_rhs - jnp.dot(
                jnp.concatenate(picks, axis=1), off_ref[level - 1, 0].reshape(kb * bs, bs), preferred_element_type=F32)
        panel = jnp.dot(partial_rhs.astype(BF16), diag_ref[level, 0], preferred_element_type=F32).astype(BF16)
        solved_ref[level, 0] = panel
        full[level, half] = panel
        if level + 1 < levels:
            stores[level][me] = panel
        if level == 0:
            pl.semaphore_wait(barrier, n)
        if level + 1 < levels:

            def send_panel(step, carry):
                panel_copy(level, lax.rem(me + step, n)).start()
                return carry

            lax.fori_loop(1, n, send_panel, 0)
        pair_copy(level).start()
        if level == 0:
            for load in loads[2:]:
                load.wait()
            inner = lax.dot_general(pred[...], train[...], CONTRACT_LAST, preferred_element_type=F32)
            inner = inner / width
            table[...] = (inner * inner).astype(BF16)
        add_level(level)

    outbox[...] = acc[...].astype(BF16)

    def sum_copy(peer):
        return pltpu.make_async_remote_copy(
            src_ref=outbox.at[peer * own_rows // block_rows], dst_ref=inbox.at[me],
            send_sem=sum_send, recv_sem=sum_recv,
            device_id={"blk": peer}, device_id_type=pl.DeviceIdType.MESH)

    inbox[me] = jnp.zeros(inbox.shape[1:], BF16)

    def send_sum(step, carry):
        sum_copy(lax.rem(me + step, n)).start()
        return carry

    lax.fori_loop(1, n, send_sum, 0)
    every = inbox.at[pl.ds(0, n - 1)]
    sums = pltpu.make_async_remote_copy(
        src_ref=every, dst_ref=every, send_sem=sum_send, recv_sem=sum_recv,
        device_id={"blk": lax.rem(me + 1, n)}, device_id_type=pl.DeviceIdType.MESH)
    for level in range(levels):
        pair_copy(level).wait_send()
        if level + 1 < levels:
            all_panels(level).wait_send()
    sums.wait_recv()
    total = acc[me * own_rows // block_rows] + jnp.sum(inbox[...].astype(F32), axis=0)
    if own_rows == block_rows:
        predicted_ref[0] = total
    else:
        pick_rows[...] = total
        predicted_ref[0] = pick_rows[pl.ds(lax.rem(me * own_rows, block_rows), own_rows)]
    sums.wait_send()


def body(rhs, diag_inv, off_blocks, columns, owner, train_desc, pred_desc):
    levels, _, rows, bs = rhs.shape
    n = lax.axis_size("blk")
    features = train_desc.shape[3]
    queries = pred_desc.shape[1]
    own_rows = queries // n
    block_rows = max(own_rows, 16)
    vmem = pl.BlockSpec(memory_space=pltpu.VMEM)
    hbm = pl.BlockSpec(memory_space=pltpu.HBM)
    solved, predicted = pl.pallas_call(
        functools.partial(kernel, n, levels),
        out_shape=(
            jax.ShapeDtypeStruct((levels, 1, rows, bs), BF16),
            jax.ShapeDtypeStruct((1, own_rows, 2 * rows), F32),
        ),
        in_specs=[hbm] * 7,
        out_specs=(vmem, vmem),
        scratch_shapes=[pltpu.VMEM((n, rows, bs), BF16) for _ in range(levels - 1)] + [
            pltpu.VMEM(rhs.shape, F32),
            pltpu.VMEM(diag_inv.shape, BF16),
            pltpu.SMEM(columns.shape, jnp.int32),
            pltpu.SMEM(owner.shape, jnp.int32),
            pltpu.VMEM(off_blocks.shape, BF16),
            pltpu.VMEM((queries, features), BF16),
            pltpu.VMEM((levels * bs, features), BF16),
            pltpu.VMEM((levels, 2, rows, bs), BF16),
            pltpu.VMEM((queries, levels * bs), BF16),
            pltpu.VMEM((queries // block_rows, block_rows, 2 * rows), F32),
            pltpu.VMEM((queries // block_rows, block_rows, 2 * rows), BF16),
            pltpu.VMEM((n, block_rows, 2 * rows), BF16),
            pltpu.VMEM((block_rows, 2 * rows), F32),
            pltpu.SemaphoreType.DMA((7,)),
            pltpu.SemaphoreType.DMA((levels,)),
            pltpu.SemaphoreType.DMA((levels,)),
            pltpu.SemaphoreType.DMA((levels,)),
            pltpu.SemaphoreType.DMA((levels,)),
            pltpu.SemaphoreType.DMA,
            pltpu.SemaphoreType.DMA,
        ],
        compiler_params=pltpu.CompilerParams(
            collective_id=0, has_side_effects=True, vmem_limit_bytes=65000 * 1024),
    )(
        rhs, diag_inv, columns, owner, off_blocks, pred_desc[0],
        train_desc.reshape(levels * bs, features),
    )
    return solved, predicted


def solution(mesh):
    placed = (
        P(None, "blk", "grp", None),
        P(None, "blk", None, None),
        P(None, "blk", None, None, None),
        P(None, "blk", None),
        P(),
        P(None, "blk", None, None),
        P("grp", None, None),
    )
    return jax.shard_map(
        body,
        mesh=mesh,
        in_specs=placed,
        out_specs=(P(None, "blk", "grp", None), P("grp", "blk", None)),
        check_vma=False,
    )
```

```python
import functools

import jax
import jax.numpy as jnp
from jax import lax
from jax.experimental import pallas as pl
from jax.experimental.pallas import tpu as pltpu
from jax.sharding import PartitionSpec as P

F32 = jnp.float32
BF16 = jnp.bfloat16
CONTRACT_LAST = (((1,), (1,)), ((), ()))


def kernel(n, plane, levels, *refs):
    operands, (solved_ref, predicted_ref), scratch = refs[:7], refs[7:9], refs[9:]
    stores = scratch[: levels - 1]
    (rhs_ref, diag_ref, columns_ref, owner_ref, off_ref, pred, train,
     full, table, acc, outbox, inbox, pick_rows,
     local_sem, send_sem, recv_sem, line_send, line_recv, pair_send, pair_recv, sum_send, sum_recv) = scratch[levels - 1:]
    me = lax.axis_index("blk")
    half = lax.axis_index("grp")
    rows, bs = rhs_ref.shape[2], rhs_ref.shape[3]
    width = train.shape[1]
    kb = columns_ref.shape[2]
    block_rows = outbox.shape[1]
    own_rows = predicted_ref.shape[1]

    here = (rhs_ref, diag_ref, columns_ref, owner_ref, off_ref, pred, train)
    loads = [pltpu.make_async_copy(operand, local, local_sem.at[i])
             for i, (operand, local) in enumerate(zip(operands, here))]
    for load in loads:
        load.start()

    barrier = pltpu.get_barrier_semaphore()

    def greet(step, carry):
        pl.semaphore_signal(barrier, inc=1, device_id={"blk": lax.rem(me + step, n)},
                            device_id_type=pl.DeviceIdType.MESH)
        return carry

    lax.fori_loop(1, n, greet, 0)
    pl.semaphore_signal(barrier, inc=1, device_id={"grp": 1 - half}, device_id_type=pl.DeviceIdType.MESH)

    line, spot = me // plane, lax.rem(me, plane)
    lines = n // plane

    def on_line(step):
        return lax.rem(line + step, lines) * plane + spot

    def in_plane(step):
        return line * plane + lax.rem(spot + step, plane)

    def panel_copy(level, block, peer, send, recv):
        return pltpu.make_async_remote_copy(
            src_ref=stores[level].at[block], dst_ref=stores[level].at[block],
            send_sem=send, recv_sem=recv, device_id={"blk": peer}, device_id_type=pl.DeviceIdType.MESH)

    def line_copy(level, step):
        return panel_copy(level, me, on_line(step), line_send.at[level, step], line_recv.at[level, step])

    def share(level, block):
        def send(step, carry):
            panel_copy(level, block, in_plane(step), send_sem.at[level], recv_sem.at[level]).start()
            return carry

        lax.fori_loop(1, plane, send, 0)

    def all_panels(level):
        every = stores[level].at[pl.ds(0, n - lines)]
        return pltpu.make_async_remote_copy(
            src_ref=every, dst_ref=every,
            send_sem=send_sem.at[level], recv_sem=recv_sem.at[level],
            device_id={"blk": in_plane(1)}, device_id_type=pl.DeviceIdType.MESH)

    def pair_copy(level):
        return pltpu.make_async_remote_copy(
            src_ref=full.at[level, half], dst_ref=full.at[level, half],
            send_sem=pair_send.at[level], recv_sem=pair_recv.at[level],
            device_id={"grp": 1 - half}, device_id_type=pl.DeviceIdType.MESH)

    def add_level(level):
        pair_copy(level).wait_recv()
        panel = full[level].reshape(2 * rows, bs)
        part = lax.dot_general(table[:, level * bs:(level + 1) * bs], panel, CONTRACT_LAST,
                               preferred_element_type=F32)
        part = part.reshape(acc.shape)
        acc[...] = part if level == 0 else acc[...] + part

    for level in range(levels):
        if level == 0:
            loads[0].wait()
            loads[1].wait()
        partial_rhs = rhs_ref[level, 0]
        if level > 0:
            all_panels(level - 1).wait_recv()
            picks = []
            for k in range(kb):
                wanted = columns_ref[level - 1, 0, k]
                from_level = wanted // n
                place = owner_ref[from_level, lax.rem(wanted, n)]
                panel = stores[0][place]
                for other in range(1, level):
                    panel = jnp.where(from_level == other, stores[other][place], panel)
                picks.append(panel)
            partial_rhs = partial_rhs - jnp.dot(
                jnp.concatenate(picks, axis=1), off_ref[level - 1, 0].reshape(kb * bs, bs), preferred_element_type=F32)
        panel = jnp.dot(partial_rhs.astype(BF16), diag_ref[level, 0], preferred_element_type=F32).astype(BF16)
        solved_ref[level, 0] = panel
        full[level, half] = panel
        if level + 1 < levels:
            stores[level][me] = panel
        if level == 0:
            pl.semaphore_wait(barrier, n)
        if level + 1 < levels:
            for step in range(1, lines):
                line_copy(level, step).start()
            share(level, me)
        pair_copy(level).start()
        if level + 1 < levels:
            for step in range(1, lines):
                line_copy(level, step).wait_recv()
                share(level, on_line(lines - step))
        if level == 0:
            for load in loads[2:]:
                load.wait()
            inner = lax.dot_general(pred[...], train[...], CONTRACT_LAST, preferred_element_type=F32)
            inner = inner / width
            table[...] = (inner * inner).astype(BF16)
        add_level(level)

    outbox[...] = acc[...].astype(BF16)

    def sum_copy(peer):
        return pltpu.make_async_remote_copy(
            src_ref=outbox.at[peer * own_rows // block_rows], dst_ref=inbox.at[me],
            send_sem=sum_send, recv_sem=sum_recv,
            device_id={"blk": peer}, device_id_type=pl.DeviceIdType.MESH)

    inbox[me] = jnp.zeros(inbox.shape[1:], BF16)

    def send_sum(step, carry):
        sum_copy(lax.rem(me + step, n)).start()
        return carry

    lax.fori_loop(1, n, send_sum, 0)
    every = inbox.at[pl.ds(0, n - 1)]
    sums = pltpu.make_async_remote_copy(
        src_ref=every, dst_ref=every, send_sem=sum_send, recv_sem=sum_recv,
        device_id={"blk": lax.rem(me + 1, n)}, device_id_type=pl.DeviceIdType.MESH)
    for level in range(levels):
        pair_copy(level).wait_send()
        if level + 1 < levels:
            all_panels(level).wait_send()
            for step in range(1, lines):
                line_copy(level, step).wait_send()
    sums.wait_recv()
    total = acc[me * own_rows // block_rows] + jnp.sum(inbox[...].astype(F32), axis=0)
    if own_rows == block_rows:
        predicted_ref[0] = total
    else:
        pick_rows[...] = total
        predicted_ref[0] = pick_rows[pl.ds(lax.rem(me * own_rows, block_rows), own_rows)]
    sums.wait_send()


def plane_of(n):
    plane = 1
    while plane * plane < n:
        plane *= 2
    return plane if n % plane == 0 else n


def body(rhs, diag_inv, off_blocks, columns, owner, train_desc, pred_desc):
    levels, _, rows, bs = rhs.shape
    n = lax.axis_size("blk")
    plane = plane_of(n)
    features = train_desc.shape[3]
    queries = pred_desc.shape[1]
    own_rows = queries // n
    block_rows = max(own_rows, 16)
    vmem = pl.BlockSpec(memory_space=pltpu.VMEM)
    hbm = pl.BlockSpec(memory_space=pltpu.HBM)
    solved, predicted = pl.pallas_call(
        functools.partial(kernel, n, plane, levels),
        out_shape=(
            jax.ShapeDtypeStruct((levels, 1, rows, bs), BF16),
            jax.ShapeDtypeStruct((1, own_rows, 2 * rows), F32),
        ),
        in_specs=[hbm] * 7,
        out_specs=(vmem, vmem),
        scratch_shapes=[pltpu.VMEM((n, rows, bs), BF16) for _ in range(levels - 1)] + [
            pltpu.VMEM(rhs.shape, F32),
            pltpu.VMEM(diag_inv.shape, BF16),
            pltpu.SMEM(columns.shape, jnp.int32),
            pltpu.SMEM(owner.shape, jnp.int32),
            pltpu.VMEM(off_blocks.shape, BF16),
            pltpu.VMEM((queries, features), BF16),
            pltpu.VMEM((levels * bs, features), BF16),
            pltpu.VMEM((levels, 2, rows, bs), BF16),
            pltpu.VMEM((queries, levels * bs), BF16),
            pltpu.VMEM((queries // block_rows, block_rows, 2 * rows), F32),
            pltpu.VMEM((queries // block_rows, block_rows, 2 * rows), BF16),
            pltpu.VMEM((n, block_rows, 2 * rows), BF16),
            pltpu.VMEM((block_rows, 2 * rows), F32),
            pltpu.SemaphoreType.DMA((7,)),
            pltpu.SemaphoreType.DMA((levels,)),
            pltpu.SemaphoreType.DMA((levels,)),
            pltpu.SemaphoreType.DMA((levels, n // plane)),
            pltpu.SemaphoreType.DMA((levels, n // plane)),
            pltpu.SemaphoreType.DMA((levels,)),
            pltpu.SemaphoreType.DMA((levels,)),
            pltpu.SemaphoreType.DMA,
            pltpu.SemaphoreType.DMA,
        ],
        compiler_params=pltpu.CompilerParams(
            collective_id=0, has_side_effects=True, vmem_limit_bytes=65000 * 1024),
    )(
        rhs, diag_inv, columns, owner, off_blocks, pred_desc[0],
        train_desc.reshape(levels * bs, features),
    )
    return solved, predicted


def solution(mesh):
    placed = (
        P(None, "blk", "grp", None),
        P(None, "blk", None, None),
        P(None, "blk", None, None, None),
        P(None, "blk", None),
        P(),
        P(None, "blk", None, None),
        P("grp", None, None),
    )
    return jax.shard_map(
        body,
        mesh=mesh,
        in_specs=placed,
        out_specs=(P(None, "blk", "grp", None), P("grp", "blk", None)),
        check_vma=False,
    )
```

```python
import functools

import jax
import jax.numpy as jnp
from jax import lax
from jax.experimental import pallas as pl
from jax.experimental.pallas import tpu as pltpu
from jax.sharding import PartitionSpec as P

F32 = jnp.float32
BF16 = jnp.bfloat16
CONTRACT_LAST = (((1,), (1,)), ((), ()))


def kernel(n, levels, *refs):
    operands, (solved_ref, predicted_ref), scratch = refs[:7], refs[7:9], refs[9:]
    stores = scratch[: levels - 1]
    (rhs_ref, diag_ref, columns_ref, owner_ref, off_ref, pred, train,
     full, table, acc, outbox, inbox, pick_rows,
     local_sem, send_sem, recv_sem, pair_send, pair_recv, sum_send, sum_recv) = scratch[levels - 1:]
    me = lax.axis_index("blk")
    half = lax.axis_index("grp")
    rows, bs = rhs_ref.shape[2], rhs_ref.shape[3]
    width = train.shape[1]
    kb = columns_ref.shape[2]
    block_rows = outbox.shape[1]
    own_rows = predicted_ref.shape[1]

    here = (rhs_ref, diag_ref, columns_ref, owner_ref, off_ref, pred, train)
    loads = [pltpu.make_async_copy(operand, local, local_sem.at[i])
             for i, (operand, local) in enumerate(zip(operands, here))]
    for load in loads:
        load.start()

    barrier = pltpu.get_barrier_semaphore()

    stride = 7 if n % 7 else 1

    def greet(step, carry):
        pl.semaphore_signal(barrier, inc=1, device_id={"blk": lax.rem(me + step, n)},
                            device_id_type=pl.DeviceIdType.MESH)
        return carry

    lax.fori_loop(1, n, greet, 0)
    pl.semaphore_signal(barrier, inc=1, device_id={"grp": 1 - half}, device_id_type=pl.DeviceIdType.MESH)

    def panel_copy(level, peer):
        return pltpu.make_async_remote_copy(
            src_ref=stores[level].at[me], dst_ref=stores[level].at[me],
            send_sem=send_sem.at[level], recv_sem=recv_sem.at[level],
            device_id={"blk": peer}, device_id_type=pl.DeviceIdType.MESH)

    def all_panels(level):
        every = stores[level].at[pl.ds(0, n - 1)]
        return pltpu.make_async_remote_copy(
            src_ref=every, dst_ref=every,
            send_sem=send_sem.at[level], recv_sem=recv_sem.at[level],
            device_id={"blk": lax.rem(me + 1, n)}, device_id_type=pl.DeviceIdType.MESH)

    def pair_copy(level):
        return pltpu.make_async_remote_copy(
            src_ref=full.at[level, half], dst_ref=full.at[level, half],
            send_sem=pair_send.at[level], recv_sem=pair_recv.at[level],
            device_id={"grp": 1 - half}, device_id_type=pl.DeviceIdType.MESH)

    def add_level(level):
        pair_copy(level).wait_recv()
        panel = full[level].reshape(2 * rows, bs)
        part = lax.dot_general(table[:, level * bs:(level + 1) * bs], panel, CONTRACT_LAST,
                               preferred_element_type=F32)
        part = part.reshape(acc.shape)
        acc[...] = part if level == 0 else acc[...] + part

    for level in range(levels):
        if level == 0:
            loads[0].wait()
            loads[1].wait()
        partial_rhs = rhs_ref[level, 0]
        if level > 0:
            all_panels(level - 1).wait_recv()
            picks = []
            for k in range(kb):
                wanted = columns_ref[level - 1, 0, k]
                from_level = wanted // n
                place = owner_ref[from_level, lax.rem(wanted, n)]
                panel = stores[0][place]
                for other in range(1, level):
                    panel = jnp.where(from_level == other, stores[other][place], panel)
                picks.append(panel)
            partial_rhs = partial_rhs - jnp.dot(
                jnp.concatenate(picks, axis=1), off_ref[level - 1, 0].reshape(kb * bs, bs), preferred_element_type=F32)
        panel = jnp.dot(partial_rhs.astype(BF16), diag_ref[level, 0], preferred_element_type=F32).astype(BF16)
        solved_ref[level, 0] = panel
        full[level, half] = panel
        if level + 1 < levels:
            stores[level][me] = panel
        if level == 0:
            pl.semaphore_wait(barrier, n)
        if level + 1 < levels:

            def send_panel(step, carry):
                panel_copy(level, lax.rem(me + step * stride, n)).start()
                return carry

            lax.fori_loop(1, n, send_panel, 0)
        pair_copy(level).start()
        if level == 0:
            for load in loads[2:]:
                load.wait()
            inner = lax.dot_general(pred[...], train[...], CONTRACT_LAST, preferred_element_type=F32)
            inner = inner / width
            table[...] = (inner * inner).astype(BF16)
        add_level(level)

    outbox[...] = acc[...].astype(BF16)

    def sum_copy(peer):
        return pltpu.make_async_remote_copy(
            src_ref=outbox.at[peer * own_rows // block_rows], dst_ref=inbox.at[me],
            send_sem=sum_send, recv_sem=sum_recv,
            device_id={"blk": peer}, device_id_type=pl.DeviceIdType.MESH)

    inbox[me] = jnp.zeros(inbox.shape[1:], BF16)

    def send_sum(step, carry):
        sum_copy(lax.rem(me + step * stride, n)).start()
        return carry

    lax.fori_loop(1, n, send_sum, 0)
    every = inbox.at[pl.ds(0, n - 1)]
    sums = pltpu.make_async_remote_copy(
        src_ref=every, dst_ref=every, send_sem=sum_send, recv_sem=sum_recv,
        device_id={"blk": lax.rem(me + 1, n)}, device_id_type=pl.DeviceIdType.MESH)
    for level in range(levels):
        pair_copy(level).wait_send()
        if level + 1 < levels:
            all_panels(level).wait_send()
    sums.wait_recv()
    total = acc[me * own_rows // block_rows] + jnp.sum(inbox[...].astype(F32), axis=0)
    if own_rows == block_rows:
        predicted_ref[0] = total
    else:
        pick_rows[...] = total
        predicted_ref[0] = pick_rows[pl.ds(lax.rem(me * own_rows, block_rows), own_rows)]
    sums.wait_send()


def store_results(solved_in, predicted_in, solved_out, predicted_out, sem):
    first = pltpu.make_async_copy(solved_in, solved_out, sem.at[0])
    second = pltpu.make_async_copy(predicted_in, predicted_out, sem.at[1])
    first.start()
    second.start()
    first.wait()
    second.wait()


def body(rhs, diag_inv, off_blocks, columns, owner, train_desc, pred_desc):
    levels, _, rows, bs = rhs.shape
    n = lax.axis_size("blk")
    features = train_desc.shape[3]
    queries = pred_desc.shape[1]
    own_rows = queries // n
    block_rows = max(own_rows, 16)
    vmem = pl.BlockSpec(memory_space=pltpu.VMEM)
    hbm = pl.BlockSpec(memory_space=pltpu.HBM)
    solved, predicted = pl.pallas_call(
        functools.partial(kernel, n, levels),
        out_shape=(
            jax.ShapeDtypeStruct((levels, 1, rows, bs), BF16),
            jax.ShapeDtypeStruct((1, own_rows, 2 * rows), F32),
        ),
        in_specs=[hbm] * 7,
        out_specs=(vmem, vmem),
        scratch_shapes=[pltpu.VMEM((n, rows, bs), BF16) for _ in range(levels - 1)] + [
            pltpu.VMEM(rhs.shape, F32),
            pltpu.VMEM(diag_inv.shape, BF16),
            pltpu.SMEM(columns.shape, jnp.int32),
            pltpu.SMEM(owner.shape, jnp.int32),
            pltpu.VMEM(off_blocks.shape, BF16),
            pltpu.VMEM((queries, features), BF16),
            pltpu.VMEM((levels * bs, features), BF16),
            pltpu.VMEM((levels, 2, rows, bs), BF16),
            pltpu.VMEM((queries, levels * bs), BF16),
            pltpu.VMEM((queries // block_rows, block_rows, 2 * rows), F32),
            pltpu.VMEM((queries // block_rows, block_rows, 2 * rows), BF16),
            pltpu.VMEM((n, block_rows, 2 * rows), BF16),
            pltpu.VMEM((block_rows, 2 * rows), F32),
            pltpu.SemaphoreType.DMA((7,)),
            pltpu.SemaphoreType.DMA((levels,)),
            pltpu.SemaphoreType.DMA((levels,)),
            pltpu.SemaphoreType.DMA((levels,)),
            pltpu.SemaphoreType.DMA((levels,)),
            pltpu.SemaphoreType.DMA,
            pltpu.SemaphoreType.DMA,
        ],
        compiler_params=pltpu.CompilerParams(
            collective_id=0, has_side_effects=True, vmem_limit_bytes=65000 * 1024),
    )(
        rhs, diag_inv, columns, owner, off_blocks, pred_desc[0],
        train_desc.reshape(levels * bs, features),
    )
    return pl.pallas_call(
        store_results,
        out_shape=(jax.ShapeDtypeStruct(solved.shape, BF16), jax.ShapeDtypeStruct(predicted.shape, F32)),
        in_specs=[vmem, vmem],
        out_specs=(hbm, hbm),
        scratch_shapes=[pltpu.SemaphoreType.DMA((2,))],
    )(solved, predicted)


def solution(mesh):
    placed = (
        P(None, "blk", "grp", None),
        P(None, "blk", None, None),
        P(None, "blk", None, None, None),
        P(None, "blk", None),
        P(),
        P(None, "blk", None, None),
        P("grp", None, None),
    )
    return jax.shard_map(
        body,
        mesh=mesh,
        in_specs=placed,
        out_specs=(P(None, "blk", "grp", None), P("grp", "blk", None)),
        check_vma=False,
    )
```

```python
import functools

import jax
import jax.numpy as jnp
from jax import lax
from jax.experimental import pallas as pl
from jax.experimental.pallas import tpu as pltpu
from jax.sharding import PartitionSpec as P

F32 = jnp.float32
BF16 = jnp.bfloat16
CONTRACT_LAST = (((1,), (1,)), ((), ()))


def kernel(n, levels, *refs):
    operands, (solved_ref, predicted_ref), scratch = refs[:7], refs[7:9], refs[9:]
    stores = scratch[: levels - 1]
    (rhs_ref, diag_ref, columns_ref, owner_ref, off_ref, pred, train,
     full, table, acc, outbox, inbox, pick_rows,
     local_sem, send_sem, recv_sem, pair_send, pair_recv, sum_send, sum_recv) = scratch[levels - 1:]
    me = lax.axis_index("blk")
    half = lax.axis_index("grp")
    rows, bs = rhs_ref.shape[2], rhs_ref.shape[3]
    width = train.shape[1]
    kb = columns_ref.shape[2]
    block_rows = outbox.shape[1]
    own_rows = predicted_ref.shape[1]

    here = (rhs_ref, diag_ref, columns_ref, owner_ref, off_ref, pred, train)
    loads = [pltpu.make_async_copy(operand, local, local_sem.at[i])
             for i, (operand, local) in enumerate(zip(operands, here))]
    for load in loads:
        load.start()

    barrier = pltpu.get_barrier_semaphore()

    stride = 7 if n % 7 else 1

    def peer_at(offset):
        return (lax.rem(me // 4 + offset // 4, n // 4) * 4 + lax.rem(lax.rem(me, 4) // 2 + lax.rem(offset, 4) // 2, 2) * 2
                + lax.rem(me + offset, 2))

    def greet(step, carry):
        pl.semaphore_signal(barrier, inc=1, device_id={"blk": lax.rem(me + step, n)},
                            device_id_type=pl.DeviceIdType.MESH)
        return carry

    lax.fori_loop(1, n, greet, 0)
    pl.semaphore_signal(barrier, inc=1, device_id={"grp": 1 - half}, device_id_type=pl.DeviceIdType.MESH)

    def panel_copy(level, peer):
        return pltpu.make_async_remote_copy(
            src_ref=stores[level].at[me], dst_ref=stores[level].at[me],
            send_sem=send_sem.at[level], recv_sem=recv_sem.at[level],
            device_id={"blk": peer}, device_id_type=pl.DeviceIdType.MESH)

    def all_panels(level):
        every = stores[level].at[pl.ds(0, n - 1)]
        return pltpu.make_async_remote_copy(
            src_ref=every, dst_ref=every,
            send_sem=send_sem.at[level], recv_sem=recv_sem.at[level],
            device_id={"blk": lax.rem(me + 1, n)}, device_id_type=pl.DeviceIdType.MESH)

    def pair_copy(level):
        return pltpu.make_async_remote_copy(
            src_ref=full.at[level, half], dst_ref=full.at[level, half],
            send_sem=pair_send.at[level], recv_sem=pair_recv.at[level],
            device_id={"grp": 1 - half}, device_id_type=pl.DeviceIdType.MESH)

    def add_level(level):
        pair_copy(level).wait_recv()
        panel = full[level].reshape(2 * rows, bs)
        part = lax.dot_general(table[:, level * bs:(level + 1) * bs], panel, CONTRACT_LAST,
                               preferred_element_type=F32)
        part = part.reshape(acc.shape)
        acc[...] = part if level == 0 else acc[...] + part

    for level in range(levels):
        if level == 0:
            loads[0].wait()
            loads[1].wait()
        partial_rhs = rhs_ref[level, 0]
        if level > 0:
            all_panels(level - 1).wait_recv()
            picks = []
            for k in range(kb):
                wanted = columns_ref[level - 1, 0, k]
                from_level = wanted // n
                place = owner_ref[from_level, lax.rem(wanted, n)]
                panel = stores[0][place]
                for other in range(1, level):
                    panel = jnp.where(from_level == other, stores[other][place], panel)
                picks.append(panel)
            partial_rhs = partial_rhs - jnp.dot(
                jnp.concatenate(picks, axis=1), off_ref[level - 1, 0].reshape(kb * bs, bs), preferred_element_type=F32)
        panel = jnp.dot(partial_rhs.astype(BF16), diag_ref[level, 0], preferred_element_type=F32).astype(BF16)
        solved_ref[level, 0] = panel
        full[level, half] = panel
        if level + 1 < levels:
            stores[level][me] = panel
        if level == 0:
            pl.semaphore_wait(barrier, n)
        if level + 1 < levels:

            def send_panel(step, carry):
                panel_copy(level, peer_at(lax.rem(step * stride, n))).start()
                return carry

            lax.fori_loop(1, n, send_panel, 0)
        pair_copy(level).start()
        if level == 0:
            for load in loads[2:]:
                load.wait()
            inner = lax.dot_general(pred[...], train[...], CONTRACT_LAST, preferred_element_type=F32)
            inner = inner / width
            table[...] = (inner * inner).astype(BF16)
        add_level(level)

    outbox[...] = acc[...].astype(BF16)

    def sum_copy(peer):
        return pltpu.make_async_remote_copy(
            src_ref=outbox.at[peer * own_rows // block_rows], dst_ref=inbox.at[me],
            send_sem=sum_send, recv_sem=sum_recv,
            device_id={"blk": peer}, device_id_type=pl.DeviceIdType.MESH)

    inbox[me] = jnp.zeros(inbox.shape[1:], BF16)

    def send_sum(step, carry):
        sum_copy(peer_at(lax.rem(step * stride, n))).start()
        return carry

    lax.fori_loop(1, n, send_sum, 0)
    every = inbox.at[pl.ds(0, n - 1)]
    sums = pltpu.make_async_remote_copy(
        src_ref=every, dst_ref=every, send_sem=sum_send, recv_sem=sum_recv,
        device_id={"blk": lax.rem(me + 1, n)}, device_id_type=pl.DeviceIdType.MESH)
    sums.wait_recv()
    total = acc[me * own_rows // block_rows] + jnp.sum(inbox[...].astype(F32), axis=0)
    if own_rows == block_rows:
        predicted_ref[0] = total
    else:
        pick_rows[...] = total
        predicted_ref[0] = pick_rows[pl.ds(lax.rem(me * own_rows, block_rows), own_rows)]
    for level in range(levels):
        pair_copy(level).wait_send()
        if level + 1 < levels:
            all_panels(level).wait_send()
    sums.wait_send()


def store_results(solved_in, predicted_in, solved_out, predicted_out, sem):
    first = pltpu.make_async_copy(solved_in, solved_out, sem.at[0])
    second = pltpu.make_async_copy(predicted_in, predicted_out, sem.at[1])
    first.start()
    second.start()
    first.wait()
    second.wait()


def body(rhs, diag_inv, off_blocks, columns, owner, train_desc, pred_desc):
    levels, _, rows, bs = rhs.shape
    n = lax.axis_size("blk")
    features = train_desc.shape[3]
    queries = pred_desc.shape[1]
    own_rows = queries // n
    block_rows = max(own_rows, 16)
    vmem = pl.BlockSpec(memory_space=pltpu.VMEM)
    hbm = pl.BlockSpec(memory_space=pltpu.HBM)
    solved, predicted = pl.pallas_call(
        functools.partial(kernel, n, levels),
        out_shape=(
            jax.ShapeDtypeStruct((levels, 1, rows, bs), BF16),
            jax.ShapeDtypeStruct((1, own_rows, 2 * rows), F32),
        ),
        in_specs=[hbm] * 7,
        out_specs=(vmem, vmem),
        scratch_shapes=[pltpu.VMEM((n, rows, bs), BF16) for _ in range(levels - 1)] + [
            pltpu.VMEM(rhs.shape, F32),
            pltpu.VMEM(diag_inv.shape, BF16),
            pltpu.SMEM(columns.shape, jnp.int32),
            pltpu.SMEM(owner.shape, jnp.int32),
            pltpu.VMEM(off_blocks.shape, BF16),
            pltpu.VMEM((queries, features), BF16),
            pltpu.VMEM((levels * bs, features), BF16),
            pltpu.VMEM((levels, 2, rows, bs), BF16),
            pltpu.VMEM((queries, levels * bs), BF16),
            pltpu.VMEM((queries // block_rows, block_rows, 2 * rows), F32),
            pltpu.VMEM((queries // block_rows, block_rows, 2 * rows), BF16),
            pltpu.VMEM((n, block_rows, 2 * rows), BF16),
            pltpu.VMEM((block_rows, 2 * rows), F32),
            pltpu.SemaphoreType.DMA((7,)),
            pltpu.SemaphoreType.DMA((levels,)),
            pltpu.SemaphoreType.DMA((levels,)),
            pltpu.SemaphoreType.DMA((levels,)),
            pltpu.SemaphoreType.DMA((levels,)),
            pltpu.SemaphoreType.DMA,
            pltpu.SemaphoreType.DMA,
        ],
        compiler_params=pltpu.CompilerParams(
            collective_id=0, has_side_effects=True, vmem_limit_bytes=65000 * 1024),
    )(
        rhs, diag_inv, columns, owner, off_blocks, pred_desc[0],
        train_desc.reshape(levels * bs, features),
    )
    return pl.pallas_call(
        store_results,
        out_shape=(jax.ShapeDtypeStruct(solved.shape, BF16), jax.ShapeDtypeStruct(predicted.shape, F32)),
        in_specs=[vmem, vmem],
        out_specs=(hbm, hbm),
        scratch_shapes=[pltpu.SemaphoreType.DMA((2,))],
    )(solved, predicted)


def solution(mesh):
    placed = (
        P(None, "blk", "grp", None),
        P(None, "blk", None, None),
        P(None, "blk", None, None, None),
        P(None, "blk", None),
        P(),
        P(None, "blk", None, None),
        P("grp", None, None),
    )
    return jax.shard_map(
        body,
        mesh=mesh,
        in_specs=placed,
        out_specs=(P(None, "blk", "grp", None), P("grp", "blk", None)),
        check_vma=False,
    )
```
